1024 devices in a mesh: dp: 32 (over y, x_lo, core), slab: 32 (over x_hi, z).
Axes of the slice: x: 8 (x_hi: 4, x_lo: 2; x = x_hi * 2 + x_lo), y: 8, z: 8, core: 2. Of those that a mesh axis runs over, the one named last changes fastest.
Arguments:
- features: bfloat16 [32, 320, 64, 256], P('dp', 'slab'), may hold values from -6 to 6
- voxel_mask: int32 [32, 320, 64], P('dp', 'slab'), may hold values 0 or 1
- block_pairs: int32 [32, 32, 27, 10], P('dp', 'slab'), may hold values from 5 to 30, as said below
- cotangent: bfloat16 [32, 320, 64, 128], P('dp', 'slab'), may hold values from -6 to 6
- weight: bfloat16 [27, 256, 128], replicated, may hold values from -0.078125 to 0.078125
Outputs:
- conv_out: bfloat16 [32, 320, 64, 128], P('dp', 'slab')
- input_grad: bfloat16 [32, 320, 64, 256], P('dp', 'slab')
- weight_grad: float32 [27, 256, 128], P(None, 'slab', 'dp')
The draws below stay inside these ranges and needn't reach their ends.
Inputs may be any that keep to these rules, and one draw needn't show every extreme that they name: `block_pairs`: entries below 10 are at least 5, so they name only the last 5 blocks of the slab below; entries from 20 to below 30 lie under 2*10 + 5, so they name only the first 5 blocks of the slab above; 30 means no block. The first slab never names a slab below it and the last never one above it.
All inputs are finite; a program needn't handle non-finite values. No bound on the sum of `voxel_mask` on one device may be relied on, other than what follows from the above.
Results may differ from the reference program's by a relative error of at most 0.0075.
Values may be sent and summed in bfloat16 or wider, within the bound.
A program may use at most 64 MiB of HBM per device.

```python
import jax
import jax.numpy as jnp
from jax import lax

C_IN = 256
C_OUT = 128
KERNEL = 27
VOX = 64
NB = 10
NH = 5
TOTAL_BLOCKS = 320
N_DP = 32
N_SLAB = 32


def draw_block_pairs(key, part):
    key = jax.random.fold_in(key, 11)
    key_own, key_low, key_up, key_gone = jax.random.split(key, 4)
    shape = (N_DP, N_SLAB, KERNEL, NB)
    own_block = jax.random.randint(key_own, shape, NB, 2 * NB)
    low_block = jax.random.randint(key_low, shape, NB - NH, NB)
    up_block = jax.random.randint(key_up, shape, 2 * NB, 2 * NB + NH)
    missing = jax.random.randint(key_gone, shape, 0, 4) == 0
    offset = jnp.arange(KERNEL)[None, None, :, None]
    side = offset // 9 - 1
    position = jnp.arange(NB)[None, None, None, :]
    slab_index = jnp.arange(N_SLAB)[None, :, None, None]
    lower_pick = jnp.where(slab_index > 0, low_block, 3 * NB)
    upper_pick = jnp.where(slab_index < N_SLAB - 1, up_block, 3 * NB)
    chosen = jnp.where((side == -1) & (position < NH), lower_pick, jnp.where((side == 1) & (position >= NB - NH), upper_pick, own_block))
    return jnp.where(missing, 3 * NB, chosen).astype(jnp.int32)


def place_ends(entries, key, least, largest):
    longest = entries.shape.index(max(entries.shape))
    spots = []
    for shift in (0, 1):
        where = [jax.random.randint(jax.random.fold_in(key, axis), (), 0, length) for axis, length in enumerate(entries.shape)]
        where[longest] = (where[longest] + shift) % entries.shape[longest]
        spots.append(tuple(where))
    return entries.at[spots[0]].set(least).at[spots[1]].set(largest)


def raised(array, key, source, target, blocks, factor):
    owner, partner = [(jnp.arange(array.shape[dim]) // (array.shape[dim] // blocks)).reshape([-1 if axis == dim else 1 for axis in range(array.ndim)]) for dim in (source, target)]
    chosen = jax.random.permutation(key, blocks)[partner]
    strong = (owner == chosen) | (owner == (partner + blocks // 2) % blocks)
    return jnp.where(strong, factor * array, array)


def block_levels(key, shape, cuts, smallest, top_value):
    factor_of = 1.0
    for axis_at, shards_of in cuts:
        steps = jax.random.uniform(jax.random.fold_in(jax.random.fold_in(key, 6), axis_at), (shards_of,), jnp.float32, smallest / len(cuts), top_value / len(cuts))
        factor_of = factor_of * jnp.repeat(jnp.exp(steps), shape[axis_at] // shards_of).reshape((-1,) + (1,) * (len(shape) - 1 - axis_at))
    return factor_of


def scatter_about(key, shape, scale, most, cuts=(), kind=jnp.bfloat16):
    array = scale * jax.random.normal(key, shape, jnp.float32)
    if cuts:
        array = array * block_levels(key, shape, cuts, -0.22, 0.18)
    return jnp.clip(array, -most, most).astype(kind)


def heavy_noise(own_key, shape, width, most, cuts, heavy, kind=jnp.bfloat16):
    entries = width * jax.random.normal(own_key, shape, jnp.float32)
    if cuts:
        entries = entries * block_levels(own_key, shape, cuts, -0.22, 0.18)
    return jnp.clip(raised(entries, jax.random.fold_in(own_key, 3), *heavy), -most, most).astype(kind)


def setup_inputs(seed: int = 0) -> dict:
    key_list = jax.random.split(jax.random.key(seed), 6)
    features = scatter_about(key_list[0], (N_DP, TOTAL_BLOCKS, VOX, C_IN), 1.0, 6.0, ((0, 32), (1, 32)))
    voxel_mask = place_ends((jax.random.randint(key_list[1], (N_DP, TOTAL_BLOCKS, VOX), 0, 4) < 3).astype(jnp.int32), jax.random.fold_in(key_list[1], 1), 0, 1)
    block_pairs = draw_block_pairs(jax.random.fold_in(key_list[5], 71), 0)
    cotangent = heavy_noise(key_list[3], (N_DP, TOTAL_BLOCKS, VOX, C_OUT), 1.0, 6.0, ((0, 32), (1, 32)), (0, 3, 32, 2.75))
    weight = scatter_about(key_list[4], (KERNEL, C_IN, C_OUT), (KERNEL * C_IN) ** -0.5, 0.078125)
    return {"features": features, "voxel_mask": voxel_mask, "block_pairs": block_pairs, "cotangent": cotangent, "weight": weight}


def reference(features, voxel_mask, block_pairs, cotangent, weight):
    total_blocks = N_SLAB * NB

    def one_group(inputs):
        feats, mask, links, grad_in = inputs
        active = mask.astype(jnp.bfloat16)[..., None]
        masked = feats * active
        padded = jnp.concatenate([masked, jnp.zeros((1, VOX, C_IN), jnp.bfloat16)], axis=0)
        base = (jnp.arange(N_SLAB, dtype=jnp.int32) * NB - NB)[:, None, None]
        global_rows = jnp.where(links == 3 * NB, total_blocks, links + base).astype(jnp.int32)
        global_rows = jnp.transpose(global_rows, (1, 0, 2)).reshape(KERNEL, total_blocks)
        masked_grad = (grad_in * active).astype(jnp.float32)

        def per_offset(carry, item):
            out_acc, adj_acc = carry
            rows, weight_k = item
            picked = padded[rows].astype(jnp.float32)
            weight_f = weight_k.astype(jnp.float32)
            out_acc = out_acc + jnp.einsum('bvc,co->bvo', picked, weight_f)
            weight_part = jnp.einsum('bvc,bvo->co', picked, masked_grad)
            adjoint = jnp.einsum('bvo,co->bvc', masked_grad, weight_f)
            adj_acc = adj_acc.at[rows].add(adjoint)
            return ((out_acc, adj_acc), weight_part)
        start = (jnp.zeros((total_blocks, VOX, C_OUT), jnp.float32), jnp.zeros((total_blocks + 1, VOX, C_IN), jnp.float32))
        (out_acc, adj_acc), weight_parts = lax.scan(per_offset, start, (global_rows, weight))
        active_f = mask.astype(jnp.float32)[..., None]
        conv = (out_acc * active_f).astype(jnp.bfloat16)
        grads = (adj_acc[:total_blocks] * active_f).astype(jnp.bfloat16)
        return (conv, grads, weight_parts)
    conv_out, input_grad, weight_parts = lax.map(one_group, (features, voxel_mask, block_pairs, cotangent))
    weight_grad = lax.optimization_barrier(jnp.sum(weight_parts, axis=0)) / jnp.sqrt(jnp.float32(N_DP * N_SLAB * NB * VOX))
    return (conv_out, input_grad, weight_grad)
```

```python
import math

import jax
import jax.numpy as jnp
from jax import lax
from jax.experimental import pallas as pl
from jax.experimental.pallas import tpu as pltpu
from jax.sharding import PartitionSpec as P

MESH = pl.DeviceIdType.MESH
F32 = jnp.float32
BF16 = jnp.bfloat16

OFFSETS = 27
BLOCKS = 10
RIM = 5
VOX = 64
CIN = 256
COUT = 128
ROWS = BLOCKS * VOX
SIDE = 8
SLOTS = 14
HALF = 7
ZERO = BLOCKS + 2 * RIM


def dot(a, b):
    return jnp.dot(a, b, preferred_element_type=F32)


def dot_nt(a, b):
    return lax.dot_general(a, b, (((1,), (1,)), ((), ())), preferred_element_type=F32)


def one_hot(rows, source):
    r = lax.broadcasted_iota(jnp.int32, (rows, rows), 0)
    c = lax.broadcasted_iota(jnp.int32, (rows, rows), 1)
    return jnp.where(c == source(r), 1.0, 0.0).astype(BF16)


def adjoint_kernel(idx, grad, weight, own, low, up, acc):
    acc[...] = jnp.zeros_like(acc)

    def step(i, carry):
        for u in range(3):
            k = i * 3 + u
            term = dot_nt(grad[...], weight[k])
            for b in range(BLOCKS):
                row = idx[k * BLOCKS + b]
                acc[row] = acc[row] + term[b * VOX : (b + 1) * VOX]
        return carry

    lax.fori_loop(0, OFFSETS // 3, step, 0)
    low[...] = acc[0:RIM].astype(BF16)
    own[...] = acc[RIM : RIM + BLOCKS]
    up[...] = acc[RIM + BLOCKS : ZERO].astype(BF16)


def main_kernel(
    idx, masked, grad, active, weight, own_adj, low_adj, up_adj,
    conv_out, input_grad, pieces,
    ext, adj_low, adj_up, grad_t, conv_acc, kept,
    core_send, core_recv, y_send, y_recv, z_send, z_recv,
    yz_send, yz_recv, zy_send, zy_recv, x_send, x_recv,
    halo_ssem, halo_rsem, core_ssem, core_rsem,
    y_ssem, y_rsem, z_ssem, z_rsem, yz_ssem, yz_rsem, zy_ssem, zy_rsem, x_ssem, x_rsem,
):
    dp = lax.axis_index("dp")
    slab = lax.axis_index("slab")
    y, x_lo, core = dp // 4, (dp // 2) % 2, dp % 2
    x_hi, z = slab // SIDE, slab % SIDE
    x = x_hi * 2 + x_lo

    def device(y, x, z, core):
        return {"dp": y * 4 + (x % 2) * 2 + core, "slab": (x // 2) * SIDE + z}

    mate = device(y, x, z, 1 - core)
    above = {"dp": dp, "slab": (slab + 1) % 32}
    below = {"dp": dp, "slab": (slab + 31) % 32}
    y_at = [(y + d) % SIDE for d in range(SIDE)]
    z_at = [(z + d) % SIDE for d in range(SIDE)]
    x_at = [(x + d) % SIDE for d in range(SIDE)]
    y_peer = [device(y_at[d], x, z, core) for d in range(SIDE)]
    z_peer = [device(y, x, z_at[d], core) for d in range(SIDE)]
    x_peer = [(x_at[d], device(y, x_at[d], z, (core + c) % 2)) for d in range(SIDE) for c in range(2)]

    barrier = pltpu.get_barrier_semaphore()
    others = [above, below] + y_peer[1:] + z_peer[1:] + [p for _, p in x_peer[1:]]
    for other in others:
        pl.semaphore_signal(barrier, inc=1, device_id=other, device_id_type=MESH)
    pl.semaphore_wait(barrier, len(others))

    def remote(src, dst, ssem, rsem, to):
        return pltpu.make_async_remote_copy(
            src_ref=src, dst_ref=dst, send_sem=ssem, recv_sem=rsem, device_id=to, device_id_type=MESH
        )

    halos = [
        remote(masked.at[pl.ds(RIM, RIM)], ext.at[pl.ds(0, RIM)], halo_ssem.at[0], halo_rsem.at[0], above),
        remote(masked.at[pl.ds(0, RIM)], ext.at[pl.ds(RIM + BLOCKS, RIM)], halo_ssem.at[1], halo_rsem.at[1], below),
        remote(low_adj, adj_up, halo_ssem.at[2], halo_rsem.at[2], below),
        remote(up_adj, adj_low, halo_ssem.at[3], halo_rsem.at[3], above),
    ]
    for copy in halos:
        copy.start()
    ext[RIM : RIM + BLOCKS] = masked[...]
    ext[ZERO] = jnp.zeros((VOX, CIN), BF16)
    grad_t[...] = dot_nt(one_hot(COUT, lambda r: r), grad[...]).astype(BF16)
    halos[0].wait_recv()
    halos[1].wait_recv()

    def picked(k, first, last):
        return jnp.concatenate([ext[idx[k * BLOCKS + b]] for b in range(first, last)], axis=0)

    def kernel_grad(k):
        total = None
        for first, last in ((0, 4), (4, 8), (8, 10)):
            part = dot(grad_t[:, first * VOX : last * VOX], picked(k, first, last))
            total = part if total is None else total + part
        return total

    def to_mate(j):
        return remote(core_send.at[j], core_recv.at[j], core_ssem.at[j], core_rsem.at[j], mate)

    def both_terms(j, carry):
        core_send[j] = kernel_grad((1 - core) * SLOTS + j).astype(BF16)
        to_mate(j).start()
        kept[j] = kernel_grad(core * SLOTS + j)
        return carry

    def chip_sum(j):
        to_mate(j).wait_recv()
        return (kept[j] + core_recv[j].astype(F32)).astype(BF16)

    lax.fori_loop(0, HALF, both_terms, 0)

    def y_slot(j, carry):
        y_send[j] = chip_sum(j)
        return carry

    lax.fori_loop(0, HALF, y_slot, 0)
    y_copy = [
        remote(
            y_send.at[:, pl.ds(pl.multiple_of(y_at[d] * 16, 16), 16), :],
            y_recv.at[d - 1], y_ssem.at[d - 1], y_rsem.at[d - 1], y_peer[d],
        )
        for d in range(1, SIDE)
    ]
    for copy in y_copy:
        copy.start()

    lax.fori_loop(HALF, SLOTS, both_terms, 0)
    by_z = one_hot(CIN, lambda r: ((r // 8) % 4) * 64 + (r // 32) * 8 + r % 8)

    def z_slot(j, carry):
        z_send[j] = dot_nt(by_z, chip_sum(j + HALF)).astype(BF16)
        return carry

    lax.fori_loop(0, HALF, z_slot, 0)
    z_copy = [
        remote(
            z_send.at[:, pl.ds(pl.multiple_of(z_at[d] * 32, 32), 32), :],
            z_recv.at[d - 1], z_ssem.at[d - 1], z_rsem.at[d - 1], z_peer[d],
        )
        for d in range(1, SIDE)
    ]
    for copy in z_copy:
        copy.start()

    conv_acc[...] = jnp.zeros_like(conv_acc)

    def conv_step(i, carry):
        for u in range(3):
            k = i * 3 + u
            conv_acc[...] = conv_acc[...] + dot(picked(k, 0, BLOCKS), weight[k])
        return carry

    lax.fori_loop(0, OFFSETS // 3, conv_step, 0)
    live = active[...].astype(F32)
    conv_out[...] = (conv_acc[...] * live).astype(BF16)

    halos[2].wait_recv()
    halos[3].wait_recv()
    for b in range(BLOCKS):
        if b < RIM:
            extra = adj_low[b]
        else:
            extra = adj_up[b - RIM]
        lb = live[b * VOX : (b + 1) * VOX]
        total = own_adj[b] + extra.astype(F32)
        input_grad[b] = (total * jnp.concatenate([lb, lb], axis=1)).astype(BF16)

    for copy in y_copy:
        copy.wait_recv()
    total = y_send[:, pl.ds(pl.multiple_of(y * 16, 16), 16), :].astype(F32)
    for d in range(1, SIDE):
        total = total + y_recv[d - 1].astype(F32)
    flat = jnp.concatenate([total.astype(BF16).reshape(HALF * 16, CIN), jnp.zeros((16, CIN), BF16)], axis=0)
    yz_send[...] = dot_nt(by_z, flat).astype(BF16)
    yz_copy = [
        remote(
            yz_send.at[pl.ds(pl.multiple_of(z_at[d] * 32, 32), 32), :],
            yz_recv.at[d - 1], yz_ssem.at[d - 1], yz_rsem.at[d - 1], z_peer[d],
        )
        for d in range(1, SIDE)
    ]
    for copy in yz_copy:
        copy.start()

    for copy in z_copy:
        copy.wait_recv()
    total = z_send[:, pl.ds(pl.multiple_of(z * 32, 32), 32), :].astype(F32)
    for d in range(1, SIDE):
        total = total + z_recv[d - 1].astype(F32)
    flat = jnp.concatenate([total.astype(BF16).reshape(HALF * 32, COUT), jnp.zeros((32, COUT), BF16)], axis=0)
    zy_send[...] = dot_nt(one_hot(COUT, lambda r: r), flat).astype(BF16)
    zy_copy = [
        remote(
            zy_send.at[pl.ds(pl.multiple_of(y_at[d] * 16, 16), 16), :],
            zy_recv.at[d - 1], zy_ssem.at[d - 1], zy_rsem.at[d - 1], y_peer[d],
        )
        for d in range(1, SIDE)
    ]
    for copy in zy_copy:
        copy.start()

    for copy in yz_copy:
        copy.wait_recv()
    first = yz_send[pl.ds(pl.multiple_of(z * 32, 32), 32), :].astype(F32)
    for d in range(1, SIDE):
        first = first + yz_recv[d - 1].astype(F32)
    for copy in zy_copy:
        copy.wait_recv()
    second = zy_send[pl.ds(pl.multiple_of(y * 16, 16), 16), :].astype(F32)
    for d in range(1, SIDE):
        second = second + zy_recv[d - 1].astype(F32)
    for i in range(SIDE):
        hi, lo = i // 2, i % 2
        x_send[i, :, 0:128] = first[hi * 8 : hi * 8 + 8]
        x_send[i, :, 128:384] = second[lo * 8 : lo * 8 + 8]
    x_copy = [
        remote(x_send.at[at], x_recv.at[n], x_ssem.at[n], x_rsem.at[n], to)
        for n, (at, to) in enumerate(x_peer[1:])
    ]
    for copy in x_copy:
        copy.start()
    for copy in x_copy:
        copy.wait_recv()
    mine = x_send[x]
    for d in range(1, SIDE):
        mine = mine + x_recv[2 * d - 1]
    theirs = x_recv[0]
    for d in range(1, SIDE):
        theirs = theirs + x_recv[2 * d]
    pieces[core] = mine
    pieces[1 - core] = theirs

    for copy in halos + y_copy + z_copy + yz_copy + zy_copy + x_copy:
        copy.wait_send()

    def sent(j, carry):
        to_mate(j).wait_send()
        return carry

    lax.fori_loop(0, SLOTS, sent, 0)


def per_device(features, voxel_mask, block_pairs, cotangent, weight):
    active = voxel_mask.reshape(BLOCKS, VOX, 1).astype(BF16)
    masked = features[0] * active
    grad = (cotangent[0] * active).reshape(ROWS, COUT)
    live = jnp.broadcast_to(active, (BLOCKS, VOX, COUT)).reshape(ROWS, COUT)
    links = block_pairs.reshape(OFFSETS * BLOCKS)
    idx = jnp.where(links == 3 * BLOCKS, ZERO, links - RIM)
    idx = jnp.concatenate([idx, jnp.full((BLOCKS,), ZERO, jnp.int32)])

    smem = pl.BlockSpec(memory_space=pltpu.SMEM)
    vmem = pl.BlockSpec(memory_space=pltpu.VMEM)
    dma = pltpu.SemaphoreType.DMA
    rim = jax.ShapeDtypeStruct((RIM, VOX, CIN), BF16)
    own, low, up = pl.pallas_call(
        adjoint_kernel,
        out_shape=(jax.ShapeDtypeStruct((BLOCKS, VOX, CIN), F32), rim, rim),
        in_specs=[smem, vmem, vmem],
        out_specs=(vmem, vmem, vmem),
        scratch_shapes=[pltpu.VMEM((ZERO + 1, VOX, CIN), F32)],
        compiler_params=pltpu.CompilerParams(vmem_limit_bytes=32 * 1024 * 1024),
        name="adjoint",
    )(idx, grad, weight)

    conv_out, input_grad, pieces = pl.pallas_call(
        main_kernel,
        out_shape=(
            jax.ShapeDtypeStruct((ROWS, COUT), BF16),
            jax.ShapeDtypeStruct((BLOCKS, VOX, CIN), BF16),
            jax.ShapeDtypeStruct((2, 8, 384), F32),
        ),
        in_specs=[smem] + [vmem] * 7,
        out_specs=(vmem, vmem, vmem),
        scratch_shapes=[
            pltpu.VMEM((ZERO + 1, VOX, CIN), BF16),
            pltpu.VMEM((RIM, VOX, CIN), BF16),
            pltpu.VMEM((RIM, VOX, CIN), BF16),
            pltpu.VMEM((COUT, ROWS), BF16),
            pltpu.VMEM((ROWS, COUT), F32),
            pltpu.VMEM((SLOTS, COUT, CIN), F32),
            pltpu.VMEM((SLOTS, COUT, CIN), BF16),
            pltpu.VMEM((SLOTS, COUT, CIN), BF16),
            pltpu.VMEM((HALF, COUT, CIN), BF16),
            pltpu.VMEM((SIDE - 1, HALF, 16, CIN), BF16),
            pltpu.VMEM((HALF, CIN, COUT), BF16),
            pltpu.VMEM((SIDE - 1, HALF, 32, COUT), BF16),
            pltpu.VMEM((CIN, 128), BF16),
            pltpu.VMEM((SIDE - 1, 32, 128), BF16),
            pltpu.VMEM((COUT, 256), BF16),
            pltpu.VMEM((SIDE - 1, 16, 256), BF16),
            pltpu.VMEM((SIDE, 8, 384), F32),
            pltpu.VMEM((15, 8, 384), F32),
            dma((4,)), dma((4,)), dma((SLOTS,)), dma((SLOTS,)),
            dma((7,)), dma((7,)), dma((7,)), dma((7,)),
            dma((7,)), dma((7,)), dma((7,)), dma((7,)),
            dma((15,)), dma((15,)),
        ],
        compiler_params=pltpu.CompilerParams(
            collective_id=0, has_side_effects=True, vmem_limit_bytes=40 * 1024 * 1024
        ),
        name="conv_and_sums",
    )(idx, masked, grad, live, weight, own, low, up)

    dp, slab = lax.axis_index("dp"), lax.axis_index("slab")
    x_lo, core, x_hi = (dp // 2) % 2, dp % 2, slab // SIDE
    by_y = pieces[:, :, :128].reshape(2, 8, 8, 2, 2, 4)
    by_y = lax.dynamic_index_in_dim(by_y, x_lo, 3, keepdims=False)
    by_y = lax.dynamic_index_in_dim(by_y, core, 3, keepdims=False)
    by_z = pieces[:, :, 128:].reshape(2, 2, 4, 8, 4, 8)
    by_z = lax.dynamic_index_in_dim(by_z, core, 1, keepdims=False)
    by_z = lax.dynamic_index_in_dim(by_z, x_hi, 3, keepdims=False)
    share = jnp.concatenate(
        [by_y.transpose(0, 2, 1, 3)[:, :HALF], by_z.transpose(0, 2, 3, 1)[:, :HALF]], axis=1
    ).reshape(2 * SLOTS, 8, 4)[:OFFSETS]
    count = lax.axis_size("dp") * lax.axis_size("slab") * ROWS
    weight_grad = share / jnp.float32(math.sqrt(count))
    return (conv_out.reshape(1, BLOCKS, VOX, COUT), input_grad[None], weight_grad)


def solution(mesh):
    placed = (
        P("dp", "slab", None, None),
        P("dp", "slab", None),
        P("dp", "slab", None, None),
        P("dp", "slab", None, None),
        P(),
    )
    return jax.shard_map(
        per_device,
        mesh=mesh,
        in_specs=placed,
        out_specs=(P("dp", "slab", None, None), P("dp", "slab", None, None), P(None, "slab", "dp")),
        check_vma=False,
    )
```

```python
import math

import jax
import jax.numpy as jnp
from jax import lax
from jax.experimental import pallas as pl
from jax.experimental.pallas import tpu as pltpu
from jax.sharding import PartitionSpec as P

MESH = pl.DeviceIdType.MESH
F32 = jnp.float32
BF16 = jnp.bfloat16

OFFSETS = 27
BLOCKS = 10
RIM = 5
VOX = 64
CIN = 256
COUT = 128
ROWS = BLOCKS * VOX
PAIRS = OFFSETS * BLOCKS
SIDE = 8
SLOTS = 14
HALF = 7
ZERO = BLOCKS + 2 * RIM
CHUNKS = ((0, 3), (3, 5), (5, 7))


def dot(a, b):
    return jnp.dot(a, b, preferred_element_type=F32)


def dot_nt(a, b):
    return lax.dot_general(a, b, (((1,), (1,)), ((), ())), preferred_element_type=F32)


def one_hot(rows, cols, match):
    r = lax.broadcasted_iota(jnp.int32, (rows, cols), 0)
    c = lax.broadcasted_iota(jnp.int32, (rows, cols), 1)
    return jnp.where(match(r, c), 1.0, 0.0).astype(BF16)


def main_kernel(
    idx, order, ends, features_hbm, mask_hbm, cotangent_hbm, weight_hbm,
    conv_hbm, input_grad_hbm, pieces,
    conv_out, input_grad, features, mask, cotangent, weight, live, ext, grad, grad_t, term, run, rim_low, rim_up, adj_low, adj_up, conv_acc,
    by_z, pick_y, pick_z, core_send, core_recv, y_send, y_recv, z_send, z_recv,
    yz_send, yz_recv, zy_send, zy_recv, x_send, x_recv,
    load_sem, out_sem, halo_ssem, halo_rsem, core_ssem, core_rsem,
    y_ssem, y_rsem, z_ssem, z_rsem, yz_ssem, yz_rsem, zy_ssem, zy_rsem, x_ssem, x_rsem,
):
    dp = lax.axis_index("dp")
    slab = lax.axis_index("slab")
    y, x_lo, core = dp // 4, (dp // 2) % 2, dp % 2
    x_hi, z = slab // SIDE, slab % SIDE
    x = x_hi * 2 + x_lo

    def device(y, x, z, core):
        return {"dp": y * 4 + (x % 2) * 2 + core, "slab": (x // 2) * SIDE + z}

    mate = device(y, x, z, 1 - core)
    above = {"dp": dp, "slab": (slab + 1) % 32}
    below = {"dp": dp, "slab": (slab + 31) % 32}
    y_at = [(y + d) % SIDE for d in range(SIDE)]
    z_at = [(z + d) % SIDE for d in range(SIDE)]
    x_at = [(x + d) % SIDE for d in range(SIDE)]
    y_peer = [device(y_at[d], x, z, core) for d in range(SIDE)]
    z_peer = [device(y, x, z_at[d], core) for d in range(SIDE)]
    x_peer = [(x_at[d], device(y, x_at[d], z, (core + c) % 2)) for d in range(SIDE) for c in range(2)]

    pairs = ((mask_hbm, mask), (features_hbm, features), (cotangent_hbm, cotangent), (weight_hbm, weight))
    loads = [pltpu.make_async_copy(src, dst, load_sem.at[n]) for n, (src, dst) in enumerate(pairs)]
    for load in loads:
        load.start()
    barrier = pltpu.get_barrier_semaphore()
    others = [above, below] + y_peer[1:] + z_peer[1:] + [p for _, p in x_peer[1:]]
    for other in others:
        pl.semaphore_signal(barrier, inc=1, device_id=other, device_id_type=MESH)

    loads[0].wait()
    loads[1].wait()
    eye = one_hot(VOX, VOX, lambda r, c: r == c)
    rows = jnp.concatenate([mask[b] for b in range(BLOCKS)], axis=0)
    columns = dot_nt(eye, rows.astype(F32).astype(BF16)).astype(BF16)
    for b in range(BLOCKS):
        spread = dot(columns, one_hot(BLOCKS, COUT, lambda r, c: r == b)).astype(BF16)
        live[b] = spread
        ext[RIM + b] = features[0, b] * jnp.concatenate([spread, spread], axis=1)
    ext[ZERO] = jnp.zeros((VOX, CIN), BF16)
    pl.semaphore_wait(barrier, len(others))

    def remote(src, dst, ssem, rsem, to):
        return pltpu.make_async_remote_copy(
            src_ref=src, dst_ref=dst, send_sem=ssem, recv_sem=rsem, device_id=to, device_id_type=MESH
        )

    halos = [
        remote(ext.at[pl.ds(BLOCKS, RIM)], ext.at[pl.ds(0, RIM)], halo_ssem.at[0], halo_rsem.at[0], above),
        remote(ext.at[pl.ds(RIM, RIM)], ext.at[pl.ds(RIM + BLOCKS, RIM)], halo_ssem.at[1], halo_rsem.at[1], below),
        remote(rim_low, adj_up, halo_ssem.at[2], halo_rsem.at[2], below),
        remote(rim_up, adj_low, halo_ssem.at[3], halo_rsem.at[3], above),
    ]
    halos[0].start()
    halos[1].start()

    loads[2].wait()
    for b in range(BLOCKS):
        grad[b * VOX : (b + 1) * VOX] = cotangent[0, b] * live[b]
    grad_t[...] = dot_nt(one_hot(COUT, COUT, lambda r, c: r == c), grad[...]).astype(BF16)
    by_z[...] = one_hot(CIN, CIN, lambda r, c: c == ((r // 8) % 4) * 64 + (r // 32) * 8 + r % 8)
    loads[3].wait()

    def term_step(i, carry):
        for u in range(3):
            k = i * 3 + u
            product = dot_nt(grad[...], weight[k]).astype(BF16)
            term[pl.ds(k * BLOCKS, BLOCKS)] = product.reshape(BLOCKS, VOX, CIN)
        return carry

    lax.fori_loop(0, OFFSETS // 3, term_step, 0)

    def run_step(i, total):
        for u in range(5):
            s = i * 5 + u
            here = order[s]
            last = order[jnp.maximum(s - 1, 0)]
            keep = jnp.where(idx[here] == idx[last], 1.0, 0.0)
            total = total * keep + term[here].astype(F32)
            run[s] = total
        return total

    lax.fori_loop(0, PAIRS // 5, run_step, jnp.zeros((VOX, CIN), F32))

    def target_sum(i):
        found = jnp.where(ends[i + 1] > ends[i], 1.0, 0.0)
        return run[jnp.maximum(ends[i + 1] - 1, 0)] * found

    for i in range(RIM):
        rim_low[i] = target_sum(i).astype(BF16)
        rim_up[i] = target_sum(RIM + BLOCKS + i).astype(BF16)
    halos[0].wait_recv()
    halos[1].wait_recv()

    def picked(k, first, last):
        return jnp.concatenate([ext[idx[k * BLOCKS + b]] for b in range(first, last)], axis=0)

    def kernel_grad(k):
        total = None
        for first, last in ((0, 4), (4, 8), (8, 10)):
            part = dot(grad_t[:, first * VOX : last * VOX], picked(k, first, last))
            total = part if total is None else total + part
        return total

    def to_mate(j):
        return remote(core_send.at[j], core_recv.at[j], core_ssem.at[j], core_rsem.at[j], mate)

    def give(j, carry):
        core_send[j] = kernel_grad((1 - core) * SLOTS + j).astype(BF16)
        to_mate(j).start()
        return carry

    for first, last in CHUNKS:
        lax.fori_loop(first, last, give, 0)
        lax.fori_loop(HALF + first, HALF + last, give, 0)

    def chip_sum(j):
        own = kernel_grad(core * SLOTS + j)
        to_mate(j).wait_recv()
        return (own + core_recv[j].astype(F32)).astype(BF16)

    def y_slot(j, carry):
        y_send[j] = chip_sum(j)
        return carry

    def z_slot(j, carry):
        z_send[j] = dot_nt(by_z[...], chip_sum(j + HALF)).astype(BF16)
        return carry

    y_copy, z_copy = [], []
    for n, (first, last) in enumerate(CHUNKS):
        part = pl.ds(first, last - first)
        lax.fori_loop(first, last, y_slot, 0)
        for d in range(1, SIDE):
            rows = pl.ds(pl.multiple_of(y_at[d] * 16, 16), 16)
            copy = remote(
                y_send.at[part, rows, :], y_recv.at[d - 1, part],
                y_ssem.at[n, d - 1], y_rsem.at[n, d - 1], y_peer[d],
            )
            copy.start()
            y_copy.append(copy)
        lax.fori_loop(first, last, z_slot, 0)
        for d in range(1, SIDE):
            rows = pl.ds(pl.multiple_of(z_at[d] * 32, 32), 32)
            copy = remote(
                z_send.at[part, rows, :], z_recv.at[d - 1, part],
                z_ssem.at[n, d - 1], z_rsem.at[n, d - 1], z_peer[d],
            )
            copy.start()
            z_copy.append(copy)
    halos[2].start()
    halos[3].start()

    conv_acc[...] = jnp.zeros_like(conv_acc)

    def conv_step(i, carry):
        for u in range(3):
            k = i * 3 + u
            conv_acc[...] = conv_acc[...] + dot(picked(k, 0, BLOCKS), weight[k])
        return carry

    lax.fori_loop(0, OFFSETS // 3, conv_step, 0)
    for b in range(BLOCKS):
        conv_out[b] = (conv_acc[b * VOX : (b + 1) * VOX] * live[b].astype(F32)).astype(BF16)
    conv_done = pltpu.make_async_copy(conv_out, conv_hbm, out_sem.at[0])
    conv_done.start()
    pick_y[...] = one_hot(
        128, 256, lambda r, c: (c % 128 < 64) & (r == ((c % 64) // 8) * 16 + (c // 128) * 8 + c % 8)
    )
    pick_z[...] = one_hot(
        256, 512, lambda r, c: (c % 128 >= 64) & (r == ((c % 64) // 8) * 32 + (c // 128) * 8 + c % 8)
    )

    for copy in y_copy:
        copy.wait_recv()
    total = y_send[:, pl.ds(pl.multiple_of(y * 16, 16), 16), :].astype(F32)
    for d in range(1, SIDE):
        total = total + y_recv[d - 1].astype(F32)
    flat = jnp.concatenate([total.astype(BF16).reshape(HALF * 16, CIN), jnp.zeros((16, CIN), BF16)], axis=0)
    yz_send[...] = dot_nt(by_z[...], flat).astype(BF16)
    yz_copy = [
        remote(
            yz_send.at[pl.ds(pl.multiple_of(z_at[d] * 32, 32), 32), :],
            yz_recv.at[d - 1], yz_ssem.at[d - 1], yz_rsem.at[d - 1], z_peer[d],
        )
        for d in range(1, SIDE)
    ]
    for copy in yz_copy:
        copy.start()

    for copy in z_copy:
        copy.wait_recv()
    total = z_send[:, pl.ds(pl.multiple_of(z * 32, 32), 32), :].astype(F32)
    for d in range(1, SIDE):
        total = total + z_recv[d - 1].astype(F32)
    flat = jnp.concatenate([total.astype(BF16).reshape(HALF * 32, COUT), jnp.zeros((32, COUT), BF16)], axis=0)
    zy_send[...] = dot_nt(one_hot(COUT, COUT, lambda r, c: r == c), flat).astype(BF16)
    zy_copy = [
        remote(
            zy_send.at[pl.ds(pl.multiple_of(y_at[d] * 16, 16), 16), :],
            zy_recv.at[d - 1], zy_ssem.at[d - 1], zy_rsem.at[d - 1], y_peer[d],
        )
        for d in range(1, SIDE)
    ]
    for copy in zy_copy:
        copy.start()

    halos[2].wait_recv()
    halos[3].wait_recv()
    for b in range(BLOCKS):
        extra = adj_low[b] if b < RIM else adj_up[b - RIM]
        lb = live[b].astype(F32)
        total = target_sum(RIM + b) + extra.astype(F32)
        input_grad[b] = (total * jnp.concatenate([lb, lb], axis=1)).astype(BF16)

    grad_done = pltpu.make_async_copy(input_grad, input_grad_hbm, out_sem.at[1])
    grad_done.start()

    for copy in yz_copy:
        copy.wait_recv()
    total = yz_send[pl.ds(pl.multiple_of(z * 32, 32), 32), :].astype(F32)
    for d in range(1, SIDE):
        total = total + yz_recv[d - 1].astype(F32)
    first = dot(total.astype(BF16), pick_y[...])
    for copy in zy_copy:
        copy.wait_recv()
    total = zy_send[pl.ds(pl.multiple_of(y * 16, 16), 16), :].astype(F32)
    for d in range(1, SIDE):
        total = total + zy_recv[d - 1].astype(F32)
    second = dot(total.astype(BF16), pick_z[...])
    for i in range(SIDE):
        hi, lo = i // 2, i % 2
        x_send[i] = (
            first[hi * 8 : hi * 8 + 8, lo * 128 : lo * 128 + 128]
            + second[lo * 8 : lo * 8 + 8, hi * 128 : hi * 128 + 128]
        )
    x_copy = [
        remote(x_send.at[at], x_recv.at[n], x_ssem.at[n], x_rsem.at[n], to)
        for n, (at, to) in enumerate(x_peer[1:])
    ]
    for copy in x_copy:
        copy.start()
    for copy in x_copy:
        copy.wait_recv()
    mine = x_send[x]
    for d in range(1, SIDE):
        mine = mine + x_recv[2 * d - 1]
    theirs = x_recv[0]
    for d in range(1, SIDE):
        theirs = theirs + x_recv[2 * d]
    pieces[core] = mine
    pieces[1 - core] = theirs

    conv_done.wait()
    grad_done.wait()
    for copy in halos + y_copy + z_copy + yz_copy + zy_copy + x_copy:
        copy.wait_send()

    def sent(j, carry):
        to_mate(j).wait_send()
        return carry

    lax.fori_loop(0, SLOTS, sent, 0)


def target_order(idx):
    number = jnp.arange(PAIRS, dtype=jnp.int32)
    key = idx * 512 + number
    rank = jnp.sum((key[None, :] < key[:, None]).astype(jnp.int32), axis=1)
    order = jnp.sum(jnp.where(rank[:, None] == number[None, :], number[:, None], 0), axis=0)
    target = jnp.arange(ZERO + 1, dtype=jnp.int32)
    ends = jnp.sum((idx[:, None] < target[None, :]).astype(jnp.int32), axis=0)
    return order, ends


def per_device(features, voxel_mask, block_pairs, cotangent, weight):
    links = block_pairs.reshape(PAIRS)
    idx = jnp.where(links == 3 * BLOCKS, ZERO, links - RIM)
    order, ends = target_order(idx)
    idx = jnp.concatenate([idx, jnp.full((BLOCKS,), ZERO, jnp.int32)])

    smem = pl.BlockSpec(memory_space=pltpu.SMEM)
    vmem = pl.BlockSpec(memory_space=pltpu.VMEM)
    hbm = pl.BlockSpec(memory_space=pltpu.HBM)
    dma = pltpu.SemaphoreType.DMA
    conv_out, input_grad, pieces = pl.pallas_call(
        main_kernel,
        out_shape=(
            jax.ShapeDtypeStruct((BLOCKS, VOX, COUT), BF16),
            jax.ShapeDtypeStruct((BLOCKS, VOX, CIN), BF16),
            jax.ShapeDtypeStruct((2, 8, 128), F32),
        ),
        in_specs=[smem] * 3 + [hbm] * 4,
        out_specs=(hbm, hbm, vmem),
        scratch_shapes=[
            pltpu.VMEM((BLOCKS, VOX, COUT), BF16),
            pltpu.VMEM((BLOCKS, VOX, CIN), BF16),
            pltpu.VMEM((1, BLOCKS, VOX, CIN), BF16),
            pltpu.VMEM((BLOCKS, 1, VOX), jnp.int32),
            pltpu.VMEM((1, BLOCKS, VOX, COUT), BF16),
            pltpu.VMEM((OFFSETS, CIN, COUT), BF16),
            pltpu.VMEM((BLOCKS, VOX, COUT), BF16),
            pltpu.VMEM((ZERO + 1, VOX, CIN), BF16),
            pltpu.VMEM((ROWS, COUT), BF16),
            pltpu.VMEM((COUT, ROWS), BF16),
            pltpu.VMEM((PAIRS, VOX, CIN), BF16),
            pltpu.VMEM((PAIRS, VOX, CIN), F32),
            pltpu.VMEM((RIM, VOX, CIN), BF16),
            pltpu.VMEM((RIM, VOX, CIN), BF16),
            pltpu.VMEM((RIM, VOX, CIN), BF16),
            pltpu.VMEM((RIM, VOX, CIN), BF16),
            pltpu.VMEM((ROWS, COUT), F32),
            pltpu.VMEM((CIN, CIN), BF16),
            pltpu.VMEM((128, 256), BF16),
            pltpu.VMEM((256, 512), BF16),
            pltpu.VMEM((SLOTS, COUT, CIN), BF16),
            pltpu.VMEM((SLOTS, COUT, CIN), BF16),
            pltpu.VMEM((HALF, COUT, CIN), BF16),
            pltpu.VMEM((SIDE - 1, HALF, 16, CIN), BF16),
            pltpu.VMEM((HALF, CIN, COUT), BF16),
            pltpu.VMEM((SIDE - 1, HALF, 32, COUT), BF16),
            pltpu.VMEM((CIN, 128), BF16),
            pltpu.VMEM((SIDE - 1, 32, 128), BF16),
            pltpu.VMEM((COUT, 256), BF16),
            pltpu.VMEM((SIDE - 1, 16, 256), BF16),
            pltpu.VMEM((SIDE, 8, 128), F32),
            pltpu.VMEM((15, 8, 128), F32),
            dma((4,)), dma((2,)), dma((4,)), dma((4,)), dma((SLOTS,)), dma((SLOTS,)),
            dma((3, 7)), dma((3, 7)), dma((3, 7)), dma((3, 7)),
            dma((7,)), dma((7,)), dma((7,)), dma((7,)),
            dma((15,)), dma((15,)),
        ],
        compiler_params=pltpu.CompilerParams(
            collective_id=0, has_side_effects=True, vmem_limit_bytes=63 * 1024 * 1024
        ),
        name="conv_and_sums",
    )(idx, order, ends, features, voxel_mask.reshape(BLOCKS, 1, VOX), cotangent, weight)

    core = lax.axis_index("dp") % 2
    by_y = lax.dynamic_index_in_dim(pieces[:, :, :64].reshape(2, 8, 8, 2, 4), core, 3, keepdims=False)
    by_z = lax.dynamic_index_in_dim(pieces[:, :, 64:].reshape(2, 2, 4, 8, 8), core, 1, keepdims=False)
    share = jnp.concatenate(
        [by_y.transpose(0, 2, 1, 3)[:, :HALF], by_z.transpose(0, 2, 3, 1)[:, :HALF]], axis=1
    ).reshape(2 * SLOTS, 8, 4)[:OFFSETS]
    count = lax.axis_size("dp") * lax.axis_size("slab") * ROWS
    weight_grad = share / jnp.float32(math.sqrt(count))
    return (conv_out[None], input_grad[None], weight_grad)


def solution(mesh):
    placed = (
        P("dp", "slab", None, None),
        P("dp", "slab", None),
        P("dp", "slab", None, None),
        P("dp", "slab", None, None),
        P(),
    )
    return jax.shard_map(
        per_device,
        mesh=mesh,
        in_specs=placed,
        out_specs=(P("dp", "slab", None, None), P("dp", "slab", None, None), P(None, "slab", "dp")),
        check_vma=False,
    )
```

```python
import math

import jax
import jax.numpy as jnp
from jax import lax
from jax.experimental import pallas as pl
from jax.experimental.pallas import tpu as pltpu
from jax.sharding import PartitionSpec as P

MESH = pl.DeviceIdType.MESH
F32 = jnp.float32
BF16 = jnp.bfloat16

OFFSETS = 27
BLOCKS = 10
RIM = 5
VOX = 64
CIN = 256
COUT = 128
ROWS = BLOCKS * VOX
PAIRS = OFFSETS * BLOCKS
SIDE = 8
SLOTS = 14
HALF = 7
ZERO = BLOCKS + 2 * RIM
CHUNKS = ((0, 3), (3, 5), (5, 7))


def dot(a, b):
    return jnp.dot(a, b, preferred_element_type=F32)


def dot_nt(a, b):
    return lax.dot_general(a, b, (((1,), (1,)), ((), ())), preferred_element_type=F32)


def one_hot(rows, cols, match):
    r = lax.broadcasted_iota(jnp.int32, (rows, cols), 0)
    c = lax.broadcasted_iota(jnp.int32, (rows, cols), 1)
    return jnp.where(match(r, c), 1.0, 0.0).astype(BF16)


def main_kernel(
    idx, order, ends, features_hbm, mask_hbm, cotangent_hbm, weight_hbm,
    conv_hbm, input_grad_hbm, pieces,
    conv_out, input_grad, features, mask, cotangent, weight, live, ext, grad, grad_t, term, run, rim_low, rim_up, adj_low, adj_up, conv_acc,
    by_z, pick_y, pick_z, core_send, core_recv, y_send, y_recv, z_send, z_recv,
    yz_send, yz_recv, zy_send, zy_recv, x_send, x_recv, x_sum, x_other,
    load_sem, out_sem, halo_ssem, halo_rsem, core_ssem, core_rsem,
    y_ssem, y_rsem, z_ssem, z_rsem, yz_ssem, yz_rsem, zy_ssem, zy_rsem, x_ssem, x_rsem,
):
    dp = lax.axis_index("dp")
    slab = lax.axis_index("slab")
    y, x_lo, core = dp // 4, (dp // 2) % 2, dp % 2
    x_hi, z = slab // SIDE, slab % SIDE
    x = x_hi * 2 + x_lo

    def device(y, x, z, core):
        return {"dp": y * 4 + (x % 2) * 2 + core, "slab": (x // 2) * SIDE + z}

    mate = device(y, x, z, 1 - core)
    above = {"dp": dp, "slab": (slab + 1) % 32}
    below = {"dp": dp, "slab": (slab + 31) % 32}
    y_at = [(y + d) % SIDE for d in range(SIDE)]
    z_at = [(z + d) % SIDE for d in range(SIDE)]
    x_at = [(x + d) % SIDE for d in range(SIDE)]
    y_peer = [device(y_at[d], x, z, core) for d in range(SIDE)]
    z_peer = [device(y, x, z_at[d], core) for d in range(SIDE)]
    x_peer = [device(y, x_at[d], z, core) for d in range(SIDE)]

    pairs = ((mask_hbm, mask), (features_hbm, features), (cotangent_hbm, cotangent), (weight_hbm, weight))
    loads = [pltpu.make_async_copy(src, dst, load_sem.at[n]) for n, (src, dst) in enumerate(pairs)]
    for load in loads:
        load.start()
    barrier = pltpu.get_barrier_semaphore()
    others = [mate, above, below] + y_peer[1:] + z_peer[1:] + x_peer[1:]
    for other in others:
        pl.semaphore_signal(barrier, inc=1, device_id=other, device_id_type=MESH)

    loads[0].wait()
    loads[1].wait()
    eye = one_hot(VOX, VOX, lambda r, c: r == c)
    rows = jnp.concatenate([mask[b] for b in range(BLOCKS)], axis=0)
    columns = dot_nt(eye, rows.astype(F32).astype(BF16)).astype(BF16)
    for b in range(BLOCKS):
        spread = dot(columns, one_hot(BLOCKS, COUT, lambda r, c: r == b)).astype(BF16)
        live[b] = spread
        ext[RIM + b] = features[0, b] * jnp.concatenate([spread, spread], axis=1)
    ext[ZERO] = jnp.zeros((VOX, CIN), BF16)
    pl.semaphore_wait(barrier, len(others))

    def remote(src, dst, ssem, rsem, to):
        return pltpu.make_async_remote_copy(
            src_ref=src, dst_ref=dst, send_sem=ssem, recv_sem=rsem, device_id=to, device_id_type=MESH
        )

    halos = [
        remote(ext.at[pl.ds(BLOCKS, RIM)], ext.at[pl.ds(0, RIM)], halo_ssem.at[0], halo_rsem.at[0], above),
        remote(ext.at[pl.ds(RIM, RIM)], ext.at[pl.ds(RIM + BLOCKS, RIM)], halo_ssem.at[1], halo_rsem.at[1], below),
        remote(rim_low, adj_up, halo_ssem.at[2], halo_rsem.at[2], below),
        remote(rim_up, adj_low, halo_ssem.at[3], halo_rsem.at[3], above),
    ]
    halos[0].start()
    halos[1].start()

    loads[2].wait()
    for b in range(BLOCKS):
        grad[b * VOX : (b + 1) * VOX] = cotangent[0, b] * live[b]
    grad_t[...] = dot_nt(one_hot(COUT, COUT, lambda r, c: r == c), grad[...]).astype(BF16)
    by_z[...] = one_hot(CIN, CIN, lambda r, c: c == ((r // 8) % 4) * 64 + (r // 32) * 8 + r % 8)
    loads[3].wait()

    def term_step(i, carry):
        for u in range(3):
            k = i * 3 + u
            product = dot_nt(grad[...], weight[k]).astype(BF16)
            term[pl.ds(k * BLOCKS, BLOCKS)] = product.reshape(BLOCKS, VOX, CIN)
        return carry

    lax.fori_loop(0, OFFSETS // 3, term_step, 0)

    def run_step(i, total):
        for u in range(5):
            s = i * 5 + u
            here = order[s]
            last = order[jnp.maximum(s - 1, 0)]
            keep = jnp.where(idx[here] == idx[last], 1.0, 0.0)
            total = total * keep + term[here].astype(F32)
            run[s] = total
        return total

    lax.fori_loop(0, PAIRS // 5, run_step, jnp.zeros((VOX, CIN), F32))

    def target_sum(i):
        found = jnp.where(ends[i + 1] > ends[i], 1.0, 0.0)
        return run[jnp.maximum(ends[i + 1] - 1, 0)] * found

    for i in range(RIM):
        rim_low[i] = target_sum(i).astype(BF16)
        rim_up[i] = target_sum(RIM + BLOCKS + i).astype(BF16)
    halos[0].wait_recv()
    halos[1].wait_recv()
    halos[2].start()
    halos[3].start()

    def picked(k, first, last):
        return jnp.concatenate([ext[idx[k * BLOCKS + b]] for b in range(first, last)], axis=0)

    def kernel_grad(k):
        total = None
        for first, last in ((0, 4), (4, 8), (8, 10)):
            part = dot(grad_t[:, first * VOX : last * VOX], picked(k, first, last))
            total = part if total is None else total + part
        return total

    def to_mate(j):
        return remote(core_send.at[j], core_recv.at[j], core_ssem.at[j], core_rsem.at[j], mate)

    def give(j, carry):
        core_send[j] = kernel_grad((1 - core) * SLOTS + j).astype(BF16)
        to_mate(j).start()
        return carry

    for first, last in CHUNKS:
        lax.fori_loop(first, last, give, 0)
        lax.fori_loop(HALF + first, HALF + last, give, 0)

    def chip_sum(j):
        own = kernel_grad(core * SLOTS + j)
        to_mate(j).wait_recv()
        return (own + core_recv[j].astype(F32)).astype(BF16)

    def y_slot(j, carry):
        y_send[j] = chip_sum(j)
        return carry

    def z_slot(j, carry):
        z_send[j] = dot_nt(by_z[...], chip_sum(j + HALF)).astype(BF16)
        return carry

    y_copy, z_copy = [], []
    for n, (first, last) in enumerate(CHUNKS):
        part = pl.ds(first, last - first)
        lax.fori_loop(first, last, y_slot, 0)
        for d in range(1, SIDE):
            rows = pl.ds(pl.multiple_of(y_at[d] * 16, 16), 16)
            copy = remote(
                y_send.at[part, rows, :], y_recv.at[d - 1, part],
                y_ssem.at[n, d - 1], y_rsem.at[n, d - 1], y_peer[d],
            )
            copy.start()
            y_copy.append(copy)
        lax.fori_loop(first, last, z_slot, 0)
        for d in range(1, SIDE):
            rows = pl.ds(pl.multiple_of(z_at[d] * 32, 32), 32)
            copy = remote(
                z_send.at[part, rows, :], z_recv.at[d - 1, part],
                z_ssem.at[n, d - 1], z_rsem.at[n, d - 1], z_peer[d],
            )
            copy.start()
            z_copy.append(copy)

    conv_acc[...] = jnp.zeros_like(conv_acc)

    def conv_step(i, carry):
        for u in range(3):
            k = i * 3 + u
            conv_acc[...] = conv_acc[...] + dot(picked(k, 0, BLOCKS), weight[k])
        return carry

    lax.fori_loop(0, OFFSETS // 3, conv_step, 0)
    for b in range(BLOCKS):
        conv_out[b] = (conv_acc[b * VOX : (b + 1) * VOX] * live[b].astype(F32)).astype(BF16)
    conv_done = pltpu.make_async_copy(conv_out, conv_hbm, out_sem.at[0])
    conv_done.start()
    pick_y[...] = one_hot(
        128, 256, lambda r, c: (c % 128 < 64) & (r == ((c % 64) // 8) * 16 + (c // 128) * 8 + c % 8)
    )
    pick_z[...] = one_hot(
        256, 512, lambda r, c: (c % 128 >= 64) & (r == ((c % 64) // 8) * 32 + (c // 128) * 8 + c % 8)
    )

    for copy in y_copy:
        copy.wait_recv()
    total = y_send[:, pl.ds(pl.multiple_of(y * 16, 16), 16), :].astype(F32)
    for d in range(1, SIDE):
        total = total + y_recv[d - 1].astype(F32)
    flat = jnp.concatenate([total.astype(BF16).reshape(HALF * 16, CIN), jnp.zeros((16, CIN), BF16)], axis=0)
    yz_send[...] = dot_nt(by_z[...], flat).astype(BF16)
    yz_copy = [
        remote(
            yz_send.at[pl.ds(pl.multiple_of(z_at[d] * 32, 32), 32), :],
            yz_recv.at[d - 1], yz_ssem.at[d - 1], yz_rsem.at[d - 1], z_peer[d],
        )
        for d in range(1, SIDE)
    ]
    for copy in yz_copy:
        copy.start()

    for copy in z_copy:
        copy.wait_recv()
    total = z_send[:, pl.ds(pl.multiple_of(z * 32, 32), 32), :].astype(F32)
    for d in range(1, SIDE):
        total = total + z_recv[d - 1].astype(F32)
    flat = jnp.concatenate([total.astype(BF16).reshape(HALF * 32, COUT), jnp.zeros((32, COUT), BF16)], axis=0)
    zy_send[...] = dot_nt(one_hot(COUT, COUT, lambda r, c: r == c), flat).astype(BF16)
    zy_copy = [
        remote(
            zy_send.at[pl.ds(pl.multiple_of(y_at[d] * 16, 16), 16), :],
            zy_recv.at[d - 1], zy_ssem.at[d - 1], zy_rsem.at[d - 1], y_peer[d],
        )
        for d in range(1, SIDE)
    ]
    for copy in zy_copy:
        copy.start()

    halos[2].wait_recv()
    halos[3].wait_recv()
    for b in range(BLOCKS):
        extra = adj_low[b] if b < RIM else adj_up[b - RIM]
        lb = live[b].astype(F32)
        total = target_sum(RIM + b) + extra.astype(F32)
        input_grad[b] = (total * jnp.concatenate([lb, lb], axis=1)).astype(BF16)

    grad_done = pltpu.make_async_copy(input_grad, input_grad_hbm, out_sem.at[1])
    grad_done.start()

    for copy in yz_copy:
        copy.wait_recv()
    total = yz_send[pl.ds(pl.multiple_of(z * 32, 32), 32), :].astype(F32)
    for d in range(1, SIDE):
        total = total + yz_recv[d - 1].astype(F32)
    first = dot(total.astype(BF16), pick_y[...])
    for copy in zy_copy:
        copy.wait_recv()
    total = zy_send[pl.ds(pl.multiple_of(y * 16, 16), 16), :].astype(F32)
    for d in range(1, SIDE):
        total = total + zy_recv[d - 1].astype(F32)
    second = dot(total.astype(BF16), pick_z[...])
    for i in range(SIDE):
        hi, lo = i // 2, i % 2
        x_send[i] = (
            first[hi * 8 : hi * 8 + 8, lo * 128 : lo * 128 + 128]
            + second[lo * 8 : lo * 8 + 8, hi * 128 : hi * 128 + 128]
        )
    x_copy = [
        remote(x_send.at[x_at[d]], x_recv.at[d - 1], x_ssem.at[d - 1], x_rsem.at[d - 1], x_peer[d])
        for d in range(1, SIDE)
    ]
    for copy in x_copy:
        copy.start()
    for copy in x_copy:
        copy.wait_recv()
    mine = x_send[x]
    for d in range(1, SIDE):
        mine = mine + x_recv[d - 1]
    x_sum[...] = mine
    swap = remote(x_sum, x_other, x_ssem.at[7], x_rsem.at[7], mate)
    swap.start()
    x_copy.append(swap)
    pieces[core] = mine
    swap.wait_recv()
    pieces[1 - core] = x_other[...]

    conv_done.wait()
    grad_done.wait()
    for copy in halos + y_copy + z_copy + yz_copy + zy_copy + x_copy:
        copy.wait_send()

    def sent(j, carry):
        to_mate(j).wait_send()
        return carry

    lax.fori_loop(0, SLOTS, sent, 0)


def target_order(idx):
    number = jnp.arange(PAIRS, dtype=jnp.int32)
    key = idx * 512 + number
    rank = jnp.sum((key[None, :] < key[:, None]).astype(jnp.int32), axis=1)
    order = jnp.sum(jnp.where(rank[:, None] == number[None, :], number[:, None], 0), axis=0)
    target = jnp.arange(ZERO + 1, dtype=jnp.int32)
    ends = jnp.sum((idx[:, None] < target[None, :]).astype(jnp.int32), axis=0)
    return order, ends


def per_device(features, voxel_mask, block_pairs, cotangent, weight):
    links = block_pairs.reshape(PAIRS)
    idx = jnp.where(links == 3 * BLOCKS, ZERO, links - RIM)
    order, ends = target_order(idx)
    idx = jnp.concatenate([idx, jnp.full((BLOCKS,), ZERO, jnp.int32)])

    smem = pl.BlockSpec(memory_space=pltpu.SMEM)
    vmem = pl.BlockSpec(memory_space=pltpu.VMEM)
    hbm = pl.BlockSpec(memory_space=pltpu.HBM)
    dma = pltpu.SemaphoreType.DMA
    conv_out, input_grad, pieces = pl.pallas_call(
        main_kernel,
        out_shape=(
            jax.ShapeDtypeStruct((BLOCKS, VOX, COUT), BF16),
            jax.ShapeDtypeStruct((BLOCKS, VOX, CIN), BF16),
            jax.ShapeDtypeStruct((2, 8, 128), F32),
        ),
        in_specs=[smem] * 3 + [hbm] * 4,
        out_specs=(hbm, hbm, vmem),
        scratch_shapes=[
            pltpu.VMEM((BLOCKS, VOX, COUT), BF16),
            pltpu.VMEM((BLOCKS, VOX, CIN), BF16),
            pltpu.VMEM((1, BLOCKS, VOX, CIN), BF16),
            pltpu.VMEM((BLOCKS, 1, VOX), jnp.int32),
            pltpu.VMEM((1, BLOCKS, VOX, COUT), BF16),
            pltpu.VMEM((OFFSETS, CIN, COUT), BF16),
            pltpu.VMEM((BLOCKS, VOX, COUT), BF16),
            pltpu.VMEM((ZERO + 1, VOX, CIN), BF16),
            pltpu.VMEM((ROWS, COUT), BF16),
            pltpu.VMEM((COUT, ROWS), BF16),
            pltpu.VMEM((PAIRS, VOX, CIN), BF16),
            pltpu.VMEM((PAIRS, VOX, CIN), F32),
            pltpu.VMEM((RIM, VOX, CIN), BF16),
            pltpu.VMEM((RIM, VOX, CIN), BF16),
            pltpu.VMEM((RIM, VOX, CIN), BF16),
            pltpu.VMEM((RIM, VOX, CIN), BF16),
            pltpu.VMEM((ROWS, COUT), F32),
            pltpu.VMEM((CIN, CIN), BF16),
            pltpu.VMEM((128, 256), BF16),
            pltpu.VMEM((256, 512), BF16),
            pltpu.VMEM((SLOTS, COUT, CIN), BF16),
            pltpu.VMEM((SLOTS, COUT, CIN), BF16),
            pltpu.VMEM((HALF, COUT, CIN), BF16),
            pltpu.VMEM((SIDE - 1, HALF, 16, CIN), BF16),
            pltpu.VMEM((HALF, CIN, COUT), BF16),
            pltpu.VMEM((SIDE - 1, HALF, 32, COUT), BF16),
            pltpu.VMEM((CIN, 128), BF16),
            pltpu.VMEM((SIDE - 1, 32, 128), BF16),
            pltpu.VMEM((COUT, 256), BF16),
            pltpu.VMEM((SIDE - 1, 16, 256), BF16),
            pltpu.VMEM((SIDE, 8, 128), F32),
            pltpu.VMEM((7, 8, 128), F32),
            pltpu.VMEM((8, 128), F32),
            pltpu.VMEM((8, 128), F32),
            dma((4,)), dma((2,)), dma((4,)), dma((4,)), dma((SLOTS,)), dma((SLOTS,)),
            dma((3, 7)), dma((3, 7)), dma((3, 7)), dma((3, 7)),
            dma((7,)), dma((7,)), dma((7,)), dma((7,)),
            dma((8,)), dma((8,)),
        ],
        compiler_params=pltpu.CompilerParams(
            collective_id=0, has_side_effects=True, vmem_limit_bytes=53 * 1024 * 1024
        ),
        name="conv_and_sums",
    )(idx, order, ends, features, voxel_mask.reshape(BLOCKS, 1, VOX), cotangent, weight)

    core = lax.axis_index("dp") % 2
    by_y = lax.dynamic_index_in_dim(pieces[:, :, :64].reshape(2, 8, 8, 2, 4), core, 3, keepdims=False)
    by_z = lax.dynamic_index_in_dim(pieces[:, :, 64:].reshape(2, 2, 4, 8, 8), core, 1, keepdims=False)
    share = jnp.concatenate(
        [by_y.transpose(0, 2, 1, 3)[:, :HALF], by_z.transpose(0, 2, 3, 1)[:, :HALF]], axis=1
    ).reshape(2 * SLOTS, 8, 4)[:OFFSETS]
    count = lax.axis_size("dp") * lax.axis_size("slab") * ROWS
    weight_grad = share / jnp.float32(math.sqrt(count))
    return (conv_out[None], input_grad[None], weight_grad)


def solution(mesh):
    placed = (
        P("dp", "slab", None, None),
        P("dp", "slab", None),
        P("dp", "slab", None, None),
        P("dp", "slab", None, None),
        P(),
    )
    return jax.shard_map(
        per_device,
        mesh=mesh,
        in_specs=placed,
        out_specs=(P("dp", "slab", None, None), P("dp", "slab", None, None), P(None, "slab", "dp")),
        check_vma=False,
    )
```
